512 devices in a mesh: ctx: 32 (over x, y, core), ch: 16 (over z).
Axes of the slice: x: 4, y: 4, z: 16, core: 2. Of those that a mesh axis runs over, the one named last changes fastest.
Arguments:
- query_gate: bfloat16 [8192, 4096], P('ctx', 'ch'), may hold values from -6 to 6
- key_gate: bfloat16 [8192, 4096], P('ctx', 'ch'), may hold values from -6 to 6
- values: bfloat16 [8192, 4096], P('ctx', 'ch'), may hold values from -6 to 6
- decay_rates: float32 [16, 4096], P(None, 'ch'), may hold values from 0 to 0.04, as said below
- residues: float32 [16, 4096], P(None, 'ch'), may hold values from -3 to 3
- skip_gain: float32 [4096], P('ch'), may hold values from 0.5 to 1.5
- out_weight: bfloat16 [4096, 4096], P(None, 'ch'), may hold values from -0.09375 to 0.09375
Outputs:
- layer_out: bfloat16 [8192, 4096], P('ctx', 'ch')
- final_state: float32 [16, 4096], P(None, ('ctx', 'ch'))
The draws below stay inside these ranges and needn't reach their ends.
Inputs may be any that keep to these rules, and one draw needn't show every extreme that they name: `decay_rates`: decay rates are positive.
All inputs are finite; a program needn't handle non-finite values.
Results may differ from the reference program's by a relative error of at most 0.0057.
Values may be sent and summed in bfloat16 or wider, within the bound.
No kernel may reach another device: no remote copies, remote signals or barrier semaphores. Data moves between devices by JAX's collectives and lax.ppermute only.
A program may use at most 128 MiB of HBM per device.

```python
import jax
import jax.numpy as jnp
from jax import lax

D = 4096
M = 16
SEQ = 8192


def draw_decay_rates(key, part):
    first = jax.random.fold_in(key, 0)
    return jnp.exp(jax.random.uniform(first, (M, D), jnp.float32, jnp.log(2.0 / SEQ), jnp.log(1.0 / 30.0)))


def levels(key, shape, pieces, least, high):
    gain, own = 1.0, jax.random.fold_in(key, 6)
    for position, blocks in pieces:
        steps = jnp.exp(jax.random.uniform(jax.random.fold_in(own, position), (blocks,), jnp.float32, least / len(pieces), high / len(pieces)))
        gain = gain * jnp.repeat(steps, shape[position] // blocks).reshape([-1 if axis == position else 1 for axis in range(len(shape))])
    return gain


def scatter_about(key, shape, spread, limit, cuts=(), held_as=jnp.bfloat16):
    values = spread * jax.random.normal(key, shape, jnp.float32)
    if cuts:
        values = values * levels(key, shape, cuts, -0.22, 0.18)
    return jnp.clip(values, -limit, limit).astype(held_as)


def setup_inputs(seed: int = 0) -> dict:
    keys = jax.random.split(jax.random.key(seed), 8)
    return {
        "query_gate": scatter_about(keys[0], (SEQ, D), 1.0, 6.0, ((0, 32), (1, 16))),
        "key_gate": scatter_about(keys[1], (SEQ, D), 1.0, 6.0, ((0, 32), (1, 16))),
        "values": scatter_about(keys[2], (SEQ, D), 1.0, 6.0, ((0, 32), (1, 16))),
        "decay_rates": draw_decay_rates(jax.random.fold_in(keys[7], 71), 0),
        "residues": scatter_about(keys[4], (M, D), 0.35, 3.0, ((1, 16),), jnp.float32),
        "skip_gain": jnp.clip(0.5 + 1.0 * jax.random.uniform(keys[5], (D,), jnp.float32) ** levels(keys[5], (D,), ((0, 16),), -0.2, 0.2), 0.5, 1.5),
        "out_weight": scatter_about(keys[6], (D, D), D ** -0.5, 0.09375, ((1, 16),)),
    }


def reference(query_gate, key_gate, values, decay_rates, residues, skip_gain, out_weight):
    gated = (key_gate.astype(jnp.float32) * values.astype(jnp.float32)).astype(jnp.bfloat16)
    amplitude = residues * jnp.sqrt(-jnp.expm1(-2.0 * decay_rates))
    signal = gated.astype(jnp.float32)
    length = signal.shape[0]
    channels = signal.shape[1]
    group = 128
    group_count = channels // group
    sig_groups = signal.reshape(length, group_count, group).transpose(1, 0, 2)
    rate_groups = decay_rates.reshape(M, group_count, group).transpose(1, 0, 2)
    amp_groups = amplitude.reshape(M, group_count, group).transpose(1, 0, 2)
    skip_groups = skip_gain.reshape(group_count, group)
    positions = jnp.arange(length).astype(jnp.float32)

    def one_group(packed):
        sig_part, rate_part, amp_part, skip_part = packed

        def add_mode(acc, pair):
            rate_row, amp_row = pair
            taps = acc + amp_row[None, :] * jnp.exp(-rate_row[None, :] * positions[:, None])
            tail = lax.optimization_barrier(jnp.sum(jnp.exp(-rate_row[None, :] * (length - 1.0 - positions)[:, None]) * sig_part, axis=0))
            return (taps, tail)
        taps, tails = lax.scan(add_mode, jnp.zeros((length, group), jnp.float32), (rate_part, amp_part))
        spectrum = jnp.fft.rfft(sig_part, n=2 * length, axis=0) * jnp.fft.rfft(taps, n=2 * length, axis=0)
        convolved = jnp.fft.irfft(spectrum, n=2 * length, axis=0)[:length]
        convolved = convolved + skip_part[None, :] * sig_part
        return (convolved, tails * amp_part)
    conv_groups, final_groups = lax.map(one_group, (sig_groups, rate_groups, amp_groups, skip_groups))
    convolved = conv_groups.transpose(1, 0, 2).reshape(length, channels)
    final_state = final_groups.transpose(1, 0, 2).reshape(M, channels)
    mixing = (query_gate.astype(jnp.float32) * convolved).astype(jnp.bfloat16)
    layer_out = jnp.dot(mixing, out_weight, preferred_element_type=jnp.float32).astype(jnp.bfloat16)
    return (layer_out, final_state)
```

```python
import functools

import jax
import jax.numpy as jnp
from jax import lax
from jax.experimental import pallas as pl
from jax.experimental.pallas import tpu as pltpu
from jax.sharding import PartitionSpec as P

F32 = jnp.float32
BF16 = jnp.bfloat16
LANES = 128
CHUNKS = 8


def row(array, index):
    return jnp.broadcast_to(array[index : index + 1], (CHUNKS, LANES))


def shifted(array, by):
    place = lax.broadcasted_iota(jnp.int32, (CHUNKS, LANES), 0)
    return jnp.where(place >= by, pltpu.roll(array, by, 0), 0.0)


def split(array):
    high = array.astype(BF16)
    return high, (array - high.astype(F32)).astype(BF16)


def local_kernel(q_ref, k_ref, v_ref, rate_ref, amplitude_ref, skip_ref, payload_ref, state_ref, u_ref, y_ref):
    tokens, channels = q_ref.shape
    modes = rate_ref.shape[0]
    steps = tokens // CHUNKS
    gated = (k_ref[...].astype(F32) * v_ref[...].astype(F32)).astype(BF16)
    u = gated.astype(F32)
    for tile in range(channels // LANES):
        lanes = slice(tile * LANES, (tile + 1) * LANES)
        u_ref[tile] = u[:, lanes]
    for tile in range(channels // LANES):
        lanes = slice(tile * LANES, (tile + 1) * LANES)
        rate = rate_ref[:, lanes]
        amplitude = amplitude_ref[:, lanes]
        pole = jnp.exp(-rate)
        poles = [row(pole, m) for m in range(modes)]
        states = [jnp.zeros((CHUNKS, LANES), F32) for _ in range(modes)]
        for step in range(steps):
            here = u_ref[tile, pl.ds(step, CHUNKS, stride=steps), :]
            states = [p * s + here for p, s in zip(poles, states)]
        for by in (1, 2, 4):
            decay = jnp.exp(-rate * float(steps * by))
            states = [s + row(decay, m) * shifted(s, by) for m, s in enumerate(states)]
        for m in range(modes):
            state_ref[m : m + 1, lanes] = amplitude[m : m + 1] * states[m][CHUNKS - 1 :]
        states = [shifted(s, 1) for s in states]
        amplitudes = [row(amplitude, m) for m in range(modes)]
        skip = jnp.broadcast_to(skip_ref[:, lanes], (CHUNKS, LANES))
        for step in range(steps):
            here = u_ref[tile, pl.ds(step, CHUNKS, stride=steps), :]
            states = [p * s + here for p, s in zip(poles, states)]
            terms = [a * s for a, s in zip(amplitudes, states)] + [skip * here]
            while len(terms) > 1:
                terms = [a + b for a, b in zip(terms[::2], terms[1::2])] + terms[len(terms) // 2 * 2 :]
            y_ref[tile, pl.ds(step, CHUNKS, stride=steps), :] = terms[0]
    payload_ref[:tokens] = q_ref[...]
    for tile in range(channels // LANES):
        payload_ref[tokens:, tile * LANES : (tile + 1) * LANES] = y_ref[tile].astype(BF16)


def prefix_kernel(tokens, place_ref, gathered_ref, rate_ref, packed_ref):
    shards, modes, channels = gathered_ref.shape
    place = place_ref[0]
    rate = rate_ref[...]
    decay = jnp.exp(-rate * float(tokens))
    running = jnp.zeros((modes, channels), F32)
    incoming = running
    for shard in range(shards):
        incoming = jnp.where(place == shard, running, incoming)
        running = decay * running + gathered_ref[shard]
    half = channels // 2
    kept = jnp.where(place % 2 == 0, running[:, :half], running[:, half:])
    for part, value in enumerate(split(incoming) + split(rate)):
        packed_ref[part * modes : (part + 1) * modes] = value
    for part, value in enumerate(split(kept)):
        packed_ref[4 * modes :, part * half : (part + 1) * half] = value


def far_kernel(modes, packed_ref, far_ref, y_ref):
    tokens, channels = far_ref.shape[1:]
    steps = tokens // CHUNKS
    start = lax.broadcasted_iota(jnp.int32, (CHUNKS, LANES), 0).astype(F32) * float(steps) + 1.0
    both = packed_ref[0].astype(F32)
    incoming = both[:modes] + both[modes : 2 * modes]
    rates = both[2 * modes : 3 * modes] + both[3 * modes : 4 * modes]
    for tile in range(channels // LANES):
        lanes = slice(tile * LANES, (tile + 1) * LANES)
        rate = rates[:, lanes]
        pole = jnp.exp(-rate)
        poles = [row(pole, m) for m in range(modes)]
        states = [row(incoming[:, lanes], m) * jnp.exp(-row(rate, m) * start) for m in range(modes)]
        for step in range(steps):
            terms = states
            while len(terms) > 1:
                terms = [a + b for a, b in zip(terms[::2], terms[1::2])]
            y_ref[tile, pl.ds(step, CHUNKS, stride=steps), :] = terms[0]
            if step < steps - 1:
                states = [p * s for p, s in zip(poles, states)]
        far_ref[0, :, lanes] = y_ref[tile]


def project_kernel(gathered_ref, far_ref, weight_ref, out_ref, total_ref):
    blocks, tokens, channels = far_ref.shape
    sums = None
    for block in range(blocks):
        q = gathered_ref[block, :tokens].astype(F32)
        near = gathered_ref[block, tokens:].astype(F32)
        mixing = (q * (near + far_ref[block])).astype(BF16)
        rows = slice(block * channels, (block + 1) * channels)
        product = jnp.dot(mixing, weight_ref[rows], preferred_element_type=F32)
        sums = product if sums is None else sums + product

    @pl.when(pl.program_id(0) == 0)
    def _():
        total_ref[...] = sums

    @pl.when(pl.program_id(0) > 0)
    def _():
        total_ref[...] += sums

    @pl.when(pl.program_id(0) == pl.num_programs(0) - 1)
    def _():
        out_ref[...] = total_ref[...].astype(BF16)


def params(mib):
    return pltpu.CompilerParams(vmem_limit_bytes=mib * 2**20)


def body(query_gate, key_gate, values, decay_rates, residues, skip_gain, out_weight):
    tokens, channels = values.shape
    modes = decay_rates.shape[0]
    ctx_total, groups = lax.axis_size("ctx"), lax.axis_size("ch")
    tiles = channels // LANES
    amplitude = residues * jnp.sqrt(-jnp.expm1(-2.0 * decay_rates))

    payload, own_state = pl.pallas_call(
        local_kernel,
        out_shape=(
            jax.ShapeDtypeStruct((2 * tokens, channels), BF16),
            jax.ShapeDtypeStruct((modes, channels), F32),
        ),
        scratch_shapes=[pltpu.VMEM((tiles, tokens, LANES), F32)] * 2,
        compiler_params=params(16),
        cost_estimate=pl.CostEstimate(flops=tokens * channels * modes * 6, bytes_accessed=2**20, transcendentals=0),
        name="local",
    )(query_gate, key_gate, values, decay_rates, amplitude, skip_gain[None, :])

    spread = lax.all_gather(payload, "ch", axis=0)
    states = lax.all_gather(own_state, "ctx", axis=0)

    place = lax.axis_index("ctx")
    packed = pl.pallas_call(
        functools.partial(prefix_kernel, tokens),
        out_shape=jax.ShapeDtypeStruct((5 * modes, channels), BF16),
        in_specs=[
            pl.BlockSpec(memory_space=pltpu.SMEM),
            pl.BlockSpec(memory_space=pltpu.VMEM),
            pl.BlockSpec(memory_space=pltpu.VMEM),
        ],
        compiler_params=params(16),
        name="prefix",
    )(place.astype(jnp.int32)[None], states, decay_rates)

    everywhere = lax.all_gather(packed, "ch", axis=0)

    far = pl.pallas_call(
        functools.partial(far_kernel, modes),
        grid=(groups,),
        out_shape=jax.ShapeDtypeStruct((groups, tokens, channels), F32),
        in_specs=[pl.BlockSpec((1, 5 * modes, channels), lambda g: (g, 0, 0))],
        out_specs=pl.BlockSpec((1, tokens, channels), lambda g: (g, 0, 0)),
        scratch_shapes=[pltpu.VMEM((tiles, tokens, LANES), F32)],
        compiler_params=params(16),
        cost_estimate=pl.CostEstimate(
            flops=groups * tokens * channels * modes * 2,
            bytes_accessed=4 * groups * tokens * channels,
            transcendentals=0,
        ),
        name="far",
    )(everywhere)

    width = channels * groups // (ctx_total * groups)
    holder = place * (channels * groups // ctx_total) // channels
    column = lax.axis_index("ch") * width
    half = channels // 2
    kept = lax.dynamic_slice(everywhere, (holder, 4 * modes, 0), (1, modes, channels))[0].astype(F32)
    kept = kept[:, :half] + kept[:, half:]
    final_state = lax.dynamic_slice(kept, (0, column), (modes, width))

    blocks = 4 if groups % 4 == 0 else 1
    layer_out = pl.pallas_call(
        project_kernel,
        grid=(groups // blocks,),
        out_shape=jax.ShapeDtypeStruct((tokens, channels), BF16),
        in_specs=[
            pl.BlockSpec((blocks, 2 * tokens, channels), lambda g: (g, 0, 0)),
            pl.BlockSpec((blocks, tokens, channels), lambda g: (g, 0, 0)),
            pl.BlockSpec((blocks * channels, channels), lambda g: (g, 0)),
        ],
        out_specs=pl.BlockSpec((tokens, channels), lambda g: (0, 0)),
        scratch_shapes=[pltpu.VMEM((tokens, channels), F32)],
        compiler_params=params(24),
        cost_estimate=pl.CostEstimate(
            flops=2 * groups * tokens * channels * channels,
            bytes_accessed=10 * groups * tokens * channels,
            transcendentals=0,
        ),
        name="project",
    )(spread, far, out_weight)
    return (layer_out, final_state)


def solution(mesh):
    return jax.shard_map(
        body,
        mesh=mesh,
        in_specs=(
            P("ctx", "ch"),
            P("ctx", "ch"),
            P("ctx", "ch"),
            P(None, "ch"),
            P(None, "ch"),
            P("ch"),
            P(None, "ch"),
        ),
        out_specs=(P("ctx", "ch"), P(None, ("ctx", "ch"))),
        check_vma=False,
    )
```

```python
import functools

import jax
import jax.numpy as jnp
from jax import lax
from jax.experimental import pallas as pl
from jax.experimental.pallas import tpu as pltpu
from jax.sharding import PartitionSpec as P

F32 = jnp.float32
BF16 = jnp.bfloat16
LANES = 128
CHUNKS = 8
WINDOW = 4
OFFSETS = (0, 1, -1, 2)


def row(array, index):
    return jnp.broadcast_to(array[index : index + 1], (CHUNKS, LANES))


def shifted(array, by):
    place = lax.broadcasted_iota(jnp.int32, (CHUNKS, LANES), 0)
    return jnp.where(place >= by, pltpu.roll(array, by, 0), 0.0)


def total(terms):
    while len(terms) > 1:
        terms = [a + b for a, b in zip(terms[::2], terms[1::2])] + terms[len(terms) // 2 * 2 :]
    return terms[0]


def gate_input(k_ref, v_ref, u_ref):
    gated = (k_ref[...].astype(F32) * v_ref[...].astype(F32)).astype(BF16).astype(F32)
    for tile in range(u_ref.shape[0]):
        u_ref[tile] = gated[:, tile * LANES : (tile + 1) * LANES]


def one_less_exp(x):
    series = jnp.ones_like(x)
    for n in range(12, 1, -1):
        series = 1.0 - x * series * (1.0 / n)
    return jnp.where(x < 0.5, x * series, 1.0 - jnp.exp(-x))


def states_kernel(k_ref, v_ref, rate_ref, state_ref, entering_ref, u_ref):
    tokens, channels = k_ref.shape
    modes = rate_ref.shape[0]
    steps = tokens // CHUNKS
    gate_input(k_ref, v_ref, u_ref)
    for tile in range(channels // LANES):
        lanes = slice(tile * LANES, (tile + 1) * LANES)
        rate = rate_ref[:, lanes]
        pole = jnp.exp(-rate)
        poles = [row(pole, m) for m in range(modes)]
        states = [jnp.zeros((CHUNKS, LANES), F32) for _ in range(modes)]
        for step in range(steps):
            here = u_ref[tile, pl.ds(step, CHUNKS, stride=steps), :]
            states = [p * s + here for p, s in zip(poles, states)]
        for by in (1, 2, 4):
            decay = jnp.exp(-rate * float(steps * by))
            states = [s + row(decay, m) * shifted(s, by) for m, s in enumerate(states)]
        for m in range(modes):
            state_ref[m : m + 1, lanes] = states[m][CHUNKS - 1 :]
            entering_ref[m, :, lanes] = shifted(states[m], 1)


def mixing_kernel(
    place_ref, q_ref, k_ref, v_ref, rate_ref, residue_ref, skip_ref, gathered_ref, entering_ref, packed_ref, u_ref, y_ref
):
    shards, modes, channels = gathered_ref.shape
    tokens = q_ref.shape[0]
    steps = tokens // CHUNKS
    place = place_ref[0]
    rates = rate_ref[...]
    amplitude = residue_ref[...] * jnp.sqrt(one_less_exp(2.0 * rates))
    decay = jnp.exp(-rates * float(tokens))
    running = jnp.zeros((modes, channels), F32)
    incoming = running
    for shard in range(shards):
        incoming = jnp.where(place == shard, running, incoming)
        running = decay * running + gathered_ref[shard]
    running = amplitude * running
    half = channels // 2
    kept = jnp.where(place % 2 == 0, running[:, :half], running[:, half:])
    high = kept.astype(BF16)
    packed_ref[tokens:, :half] = high
    packed_ref[tokens:, half:] = (kept - high.astype(F32)).astype(BF16)

    gate_input(k_ref, v_ref, u_ref)
    before = lax.broadcasted_iota(jnp.int32, (CHUNKS, LANES), 0).astype(F32) * float(steps)
    for tile in range(channels // LANES):
        lanes = slice(tile * LANES, (tile + 1) * LANES)
        rate = rates[:, lanes]
        pole = jnp.exp(-rate)
        poles = [row(pole, m) for m in range(modes)]
        amplitudes = [row(amplitude[:, lanes], m) for m in range(modes)]
        states = [
            entering_ref[m, :, lanes] + row(incoming[:, lanes], m) * jnp.exp(-row(rate, m) * before)
            for m in range(modes)
        ]
        skip = jnp.broadcast_to(skip_ref[:, lanes], (CHUNKS, LANES))
        for step in range(steps):
            here = u_ref[tile, pl.ds(step, CHUNKS, stride=steps), :]
            states = [p * s + here for p, s in zip(poles, states)]
            y = total([a * s for a, s in zip(amplitudes, states)] + [skip * here])
            y_ref[tile, pl.ds(step, CHUNKS, stride=steps), :] = y
        packed_ref[:tokens, lanes] = (q_ref[:, lanes].astype(F32) * y_ref[tile]).astype(BF16)


def project_kernel(width, place_ref, *refs):
    blocks, weights = refs[: len(OFFSETS)], refs[len(OFFSETS) : 2 * len(OFFSETS)]
    out_ref, final_ref, total_ref = refs[2 * len(OFFSETS) :]
    tokens, channels = out_ref.shape
    half = channels // 2
    step = pl.program_id(0)
    sums = total(
        [jnp.dot(b[0, :tokens], w[...], preferred_element_type=F32) for b, w in zip(blocks, weights)]
    )

    @pl.when(step == 0)
    def _():
        total_ref[...] = sums

    @pl.when(step > 0)
    def _():
        total_ref[...] += sums

    @pl.when(step == pl.num_programs(0) - 1)
    def _():
        out_ref[...] = total_ref[...].astype(BF16)

    holder = place_ref[0] // 2
    for block, offset in zip(blocks, OFFSETS):
        from_class = (place_ref[1] + offset + WINDOW) % WINDOW

        @pl.when((holder % WINDOW == from_class) & (holder // WINDOW == step))
        def _():
            kept = block[0, tokens:, :half].astype(F32) + block[0, tokens:, half:].astype(F32)
            column = place_ref[1] * width
            final_ref[...] = pltpu.roll(kept, (half - column) % half, 1)[:, :width]


def params(mib):
    return pltpu.CompilerParams(vmem_limit_bytes=mib * 2**20)


def body(query_gate, key_gate, values, decay_rates, residues, skip_gain, out_weight):
    tokens, channels = values.shape
    modes = decay_rates.shape[0]
    ctx_total, groups = lax.axis_size("ctx"), lax.axis_size("ch")
    tiles = channels // LANES
    members = groups // WINDOW
    width = channels // ctx_total
    assert ctx_total == 2 * groups and channels == 2 * LANES
    place = jnp.stack([lax.axis_index("ctx"), lax.axis_index("ch")]).astype(jnp.int32)
    whole = pl.BlockSpec(memory_space=pltpu.VMEM)
    scratch = pltpu.VMEM((tiles, tokens, LANES), F32)

    own_state, entering = pl.pallas_call(
        states_kernel,
        out_shape=(
            jax.ShapeDtypeStruct((modes, channels), F32),
            jax.ShapeDtypeStruct((modes, CHUNKS, channels), F32),
        ),
        scratch_shapes=[scratch],
        compiler_params=params(56),
        name="states",
    )(key_gate, values, decay_rates)

    gathered = lax.all_gather(own_state, "ctx", axis=0)

    packed = pl.pallas_call(
        mixing_kernel,
        out_shape=jax.ShapeDtypeStruct((tokens + modes, channels), BF16),
        in_specs=[pl.BlockSpec(memory_space=pltpu.SMEM)] + [whole] * 8,
        scratch_shapes=[scratch, scratch],
        compiler_params=params(56),
        name="mixing",
    )(place, query_gate, key_gate, values, decay_rates, residues, skip_gain[None, :], gathered, entering)

    far = [[one + WINDOW * member for member in range(members)] for one in range(WINDOW)]
    own = lax.all_gather(packed, "ch", axis=0, axis_index_groups=far)
    window = [own] + [
        lax.ppermute(own, "ch", [(i, (i - offset) % groups) for i in range(groups)]) for offset in OFFSETS[1:]
    ]

    def weight_spec(offset):
        return pl.BlockSpec(
            (channels, channels), lambda g, s: ((s[1] + offset + WINDOW) % WINDOW + WINDOW * g, 0)
        )

    layer_out, final_state = pl.pallas_call(
        functools.partial(project_kernel, width),
        grid_spec=pltpu.PrefetchScalarGridSpec(
            num_scalar_prefetch=1,
            grid=(members,),
            in_specs=[pl.BlockSpec((1, tokens + modes, channels), lambda g, s: (g, 0, 0)) for _ in OFFSETS]
            + [weight_spec(offset) for offset in OFFSETS],
            out_specs=(
                pl.BlockSpec((tokens, channels), lambda g, s: (0, 0)),
                pl.BlockSpec((modes, width), lambda g, s: (0, 0)),
            ),
            scratch_shapes=[pltpu.VMEM((tokens, channels), F32)],
        ),
        out_shape=(
            jax.ShapeDtypeStruct((tokens, channels), BF16),
            jax.ShapeDtypeStruct((modes, width), F32),
        ),
        compiler_params=params(56),
        name="project",
    )(place, *window, *[out_weight] * len(OFFSETS))
    return (layer_out, final_state)


def solution(mesh):
    return jax.shard_map(
        body,
        mesh=mesh,
        in_specs=(
            P("ctx", "ch"),
            P("ctx", "ch"),
            P("ctx", "ch"),
            P(None, "ch"),
            P(None, "ch"),
            P("ch"),
            P(None, "ch"),
        ),
        out_specs=(P("ctx", "ch"), P(None, ("ctx", "ch"))),
        check_vma=False,
    )
```

```python
import functools

import jax
import jax.numpy as jnp
from jax import lax
from jax.experimental import pallas as pl
from jax.experimental.pallas import tpu as pltpu
from jax.sharding import PartitionSpec as P

F32 = jnp.float32
BF16 = jnp.bfloat16
LANES = 128
CHUNKS = 8
WINDOW = 4


def row(array, index):
    return jnp.broadcast_to(array[index : index + 1], (CHUNKS, LANES))


def shifted(array, by):
    place = lax.broadcasted_iota(jnp.int32, (CHUNKS, LANES), 0)
    return jnp.where(place >= by, pltpu.roll(array, by, 0), 0.0)


def total(terms):
    while len(terms) > 1:
        terms = [a + b for a, b in zip(terms[::2], terms[1::2])] + terms[len(terms) // 2 * 2 :]
    return terms[0]


def gate_input(k_ref, v_ref, u_ref):
    gated = (k_ref[...].astype(F32) * v_ref[...].astype(F32)).astype(BF16).astype(F32)
    for tile in range(u_ref.shape[0]):
        u_ref[tile] = gated[:, tile * LANES : (tile + 1) * LANES]


def one_less_exp(x):
    series = jnp.ones_like(x)
    for n in range(12, 1, -1):
        series = 1.0 - x * series * (1.0 / n)
    return jnp.where(x < 0.5, x * series, 1.0 - jnp.exp(-x))


def states_kernel(k_ref, v_ref, rate_ref, state_ref, entering_ref, u_ref):
    tokens, channels = k_ref.shape
    modes = rate_ref.shape[0]
    steps = tokens // CHUNKS
    gate_input(k_ref, v_ref, u_ref)
    for tile in range(channels // LANES):
        lanes = slice(tile * LANES, (tile + 1) * LANES)
        rate = rate_ref[:, lanes]
        pole = jnp.exp(-rate)
        poles = [row(pole, m) for m in range(modes)]
        states = [jnp.zeros((CHUNKS, LANES), F32) for _ in range(modes)]
        for step in range(steps):
            here = u_ref[tile, pl.ds(step, CHUNKS, stride=steps), :]
            states = [p * s + here for p, s in zip(poles, states)]
        for by in (1, 2, 4):
            decay = jnp.exp(-rate * float(steps * by))
            states = [s + row(decay, m) * shifted(s, by) for m, s in enumerate(states)]
        for m in range(modes):
            state_ref[m : m + 1, lanes] = states[m][CHUNKS - 1 :]
            entering_ref[m, :, lanes] = shifted(states[m], 1)


def mixing_kernel(
    q_ref, k_ref, v_ref, rate_ref, residue_ref, skip_ref, gathered_ref, entering_ref, packed_ref, u_ref, y_ref
):
    shards, modes, channels = gathered_ref.shape
    tokens = q_ref.shape[0]
    steps = tokens // CHUNKS
    place = lax.axis_index("ctx")
    rates = rate_ref[...]
    amplitude = residue_ref[...] * jnp.sqrt(one_less_exp(2.0 * rates))
    decay = jnp.exp(-rates * float(tokens))
    running = jnp.zeros((modes, channels), F32)
    incoming = running
    for shard in range(shards):
        incoming = jnp.where(place == shard, running, incoming)
        running = decay * running + gathered_ref[shard]
    running = amplitude * running
    half = channels // 2
    kept = jnp.where(place % 2 == 0, running[:, :half], running[:, half:])
    high = kept.astype(BF16)
    packed_ref[tokens:, :half] = high
    packed_ref[tokens:, half:] = (kept - high.astype(F32)).astype(BF16)

    gate_input(k_ref, v_ref, u_ref)
    before = lax.broadcasted_iota(jnp.int32, (CHUNKS, LANES), 0).astype(F32) * float(steps)
    for tile in range(channels // LANES):
        lanes = slice(tile * LANES, (tile + 1) * LANES)
        rate = rates[:, lanes]
        pole = jnp.exp(-rate)
        poles = [row(pole, m) for m in range(modes)]
        amplitudes = [row(amplitude[:, lanes], m) for m in range(modes)]
        states = [
            entering_ref[m, :, lanes] + row(incoming[:, lanes], m) * jnp.exp(-row(rate, m) * before)
            for m in range(modes)
        ]
        skip = jnp.broadcast_to(skip_ref[:, lanes], (CHUNKS, LANES))
        for step in range(steps):
            here = u_ref[tile, pl.ds(step, CHUNKS, stride=steps), :]
            states = [p * s + here for p, s in zip(poles, states)]
            y = total([a * s for a, s in zip(amplitudes, states)] + [skip * here])
            y_ref[tile, pl.ds(step, CHUNKS, stride=steps), :] = y
        packed_ref[:tokens, lanes] = (q_ref[:, lanes].astype(F32) * y_ref[tile]).astype(BF16)


def project_kernel(width, parts, has_total, *refs):
    count = len(parts)
    blocks, weight_ref = refs[:count], refs[count]
    refs = refs[count + 1 :]
    if has_total:
        total_in_ref, final_in_ref, *refs = refs
    out_ref, final_ref, rows_ref, sems = refs
    tokens, channels = out_ref.shape
    half = channels // 2
    modes = blocks[0].shape[1] - tokens
    group = lax.axis_index("ch")
    copies = []
    for offset, first, number in parts:
        start = lax.rem(group + (offset + WINDOW), WINDOW)
        for member in range(first, first + number):
            at = len(copies)
            copy = pltpu.make_async_copy(
                weight_ref.at[pl.ds(pl.multiple_of((start + WINDOW * member) * channels, channels), channels)],
                rows_ref.at[at],
                sems.at[at],
            )
            copy.start()
            copies.append(copy)

    holder = lax.axis_index("ctx") // 2
    picked = jnp.zeros((width, modes), F32)
    for block, (offset, first, number) in zip(blocks, parts):
        here = lax.rem(group + (offset + WINDOW), WINDOW) == lax.rem(holder, WINDOW)
        slot = holder // WINDOW - first
        here = here & (slot >= 0) & (slot < number)
        kept = block[jnp.clip(slot, 0, number - 1), tokens:, :]
        line = lax.broadcasted_iota(jnp.int32, (width, half), 0)
        lane = lax.broadcasted_iota(jnp.int32, (width, half), 1)
        chosen = jnp.where((lane == line + group * width) & here, 1.0, 0.0).astype(BF16)
        for side in (kept[:, :half], kept[:, half:]):
            picked += lax.dot_general(chosen, side, (((1,), (1,)), ((), ())), preferred_element_type=F32)
    final_ref[...] = final_in_ref[...] + picked if has_total else picked

    sums = [total_in_ref[...]] if has_total else []
    at = 0
    for block, (_, _, number) in zip(blocks, parts):
        for member in range(number):
            copies[at].wait()
            sums.append(jnp.dot(block[member, :tokens], rows_ref[at], preferred_element_type=F32))
            at += 1
            if len(sums) > 1:
                sums = [sums[0] + sums[1]]
    out_ref[...] = sums[0].astype(out_ref.dtype)


def project(width, modes, parts, blocks, weight, before=(), last=False):
    channels = weight.shape[1]
    tokens = blocks[0].shape[1] - modes
    number = sum(part[2] for part in parts)
    whole = pl.BlockSpec(memory_space=pltpu.VMEM)
    return pl.pallas_call(
        functools.partial(project_kernel, width, parts, bool(before)),
        out_shape=(
            jax.ShapeDtypeStruct((tokens, channels), BF16 if last else F32),
            jax.ShapeDtypeStruct((width, modes), F32),
        ),
        in_specs=[whole] * len(blocks) + [pl.BlockSpec(memory_space=pl.ANY)] + [whole] * len(before),
        out_specs=(whole, whole),
        scratch_shapes=[
            pltpu.VMEM((number, channels, channels), BF16),
            pltpu.SemaphoreType.DMA((number,)),
        ],
        compiler_params=params(16),
        cost_estimate=pl.CostEstimate(
            flops=2 * number * tokens * channels * channels,
            bytes_accessed=8 * number * tokens * channels,
            transcendentals=0,
        ),
        name="project",
    )(*blocks, weight, *before)


def params(mib):
    return pltpu.CompilerParams(vmem_limit_bytes=mib * 2**20)


def body(query_gate, key_gate, values, decay_rates, residues, skip_gain, out_weight):
    tokens, channels = values.shape
    modes = decay_rates.shape[0]
    ctx_total, groups = lax.axis_size("ctx"), lax.axis_size("ch")
    tiles = channels // LANES
    members = groups // WINDOW
    width = channels // ctx_total
    assert ctx_total == 2 * groups and channels == 2 * LANES and members >= 2
    scratch = pltpu.VMEM((tiles, tokens, LANES), F32)

    own_state, entering = pl.pallas_call(
        states_kernel,
        out_shape=(
            jax.ShapeDtypeStruct((modes, channels), F32),
            jax.ShapeDtypeStruct((modes, CHUNKS, channels), F32),
        ),
        scratch_shapes=[scratch],
        compiler_params=params(56),
        name="states",
    )(key_gate, values, decay_rates)

    gathered = lax.all_gather(own_state, "ctx", axis=0)

    packed = pl.pallas_call(
        mixing_kernel,
        out_shape=jax.ShapeDtypeStruct((tokens + modes, channels), BF16),
        scratch_shapes=[scratch, scratch],
        compiler_params=params(56),
        name="mixing",
    )(query_gate, key_gate, values, decay_rates, residues, skip_gain[None, :], gathered, entering)

    far = [[one + WINDOW * member for member in range(members)] for one in range(WINDOW)]
    own = lax.all_gather(packed, "ch", axis=0, axis_index_groups=far)

    def arrive(array, offset):
        return lax.ppermute(array, "ch", [(i, (i - offset) % groups) for i in range(groups)])

    above, below = arrive(own, 1), arrive(own, -1)
    run = functools.partial(project, width, modes)
    one = run(((0, 0, members),), (own,), out_weight)
    cut = members // 2
    low, high = arrive(above[:cut], 1), arrive(below[cut:], -1)
    two = run(((1, 0, members), (-1, 0, members)), (above, below), out_weight, one)
    layer_out, final_state = run(
        ((2, 0, cut), (2, cut, members - cut)), (low, high), out_weight, two, last=True
    )
    return (layer_out, final_state.T)


def solution(mesh):
    return jax.shard_map(
        body,
        mesh=mesh,
        in_specs=(
            P("ctx", "ch"),
            P("ctx", "ch"),
            P("ctx", "ch"),
            P(None, "ch"),
            P(None, "ch"),
            P("ch"),
            P(None, "ch"),
        ),
        out_specs=(P("ctx", "ch"), P(None, ("ctx", "ch"))),
        check_vma=False,
    )
```

```python
import functools

import jax
import jax.numpy as jnp
from jax import lax
from jax.experimental import pallas as pl
from jax.experimental.pallas import tpu as pltpu
from jax.sharding import PartitionSpec as P

F32 = jnp.float32
BF16 = jnp.bfloat16
LANES = 128
CHUNKS = 8
WINDOW = 4


def row(array, index):
    return jnp.broadcast_to(array[index : index + 1], (CHUNKS, LANES))


def shifted(array, by):
    place = lax.broadcasted_iota(jnp.int32, (CHUNKS, LANES), 0)
    return jnp.where(place >= by, pltpu.roll(array, by, 0), 0.0)


def total(terms):
    while len(terms) > 1:
        terms = [a + b for a, b in zip(terms[::2], terms[1::2])] + terms[len(terms) // 2 * 2 :]
    return terms[0]


def gate_input(k_ref, v_ref, u_ref):
    gated = (k_ref[...].astype(F32) * v_ref[...].astype(F32)).astype(BF16).astype(F32)
    for tile in range(u_ref.shape[0]):
        u_ref[tile] = gated[:, tile * LANES : (tile + 1) * LANES]


def one_less_exp(x):
    series = jnp.ones_like(x)
    for n in range(12, 1, -1):
        series = 1.0 - x * series * (1.0 / n)
    return jnp.where(x < 0.5, x * series, 1.0 - jnp.exp(-x))


def states_kernel(k_ref, v_ref, rate_ref, state_ref, entering_ref, u_ref):
    tokens, channels = k_ref.shape
    modes = rate_ref.shape[0]
    steps = tokens // CHUNKS
    gate_input(k_ref, v_ref, u_ref)
    for tile in range(channels // LANES):
        lanes = slice(tile * LANES, (tile + 1) * LANES)
        rate = rate_ref[:, lanes]
        pole = jnp.exp(-rate)
        poles = [row(pole, m) for m in range(modes)]
        states = [jnp.zeros((CHUNKS, LANES), F32) for _ in range(modes)]
        for step in range(steps):
            here = u_ref[tile, pl.ds(step, CHUNKS, stride=steps), :]
            states = [p * s + here for p, s in zip(poles, states)]
        for by in (1, 2, 4):
            decay = jnp.exp(-rate * float(steps * by))
            states = [s + row(decay, m) * shifted(s, by) for m, s in enumerate(states)]
        for m in range(modes):
            state_ref[m : m + 1, lanes] = states[m][CHUNKS - 1 :]
            entering_ref[m, :, lanes] = shifted(states[m], 1)


def mixing_kernel(
    q_ref, k_ref, v_ref, rate_ref, residue_ref, skip_ref, gathered_ref, entering_ref, packed_ref, u_ref, y_ref
):
    shards, modes, channels = gathered_ref.shape
    tokens = q_ref.shape[0]
    steps = tokens // CHUNKS
    place = lax.axis_index("ctx")
    rates = rate_ref[...]
    amplitude = residue_ref[...] * jnp.sqrt(one_less_exp(2.0 * rates))
    decay = jnp.exp(-rates * float(tokens))
    running = jnp.zeros((modes, channels), F32)
    incoming = running
    for shard in range(shards):
        incoming = jnp.where(place == shard, running, incoming)
        running = decay * running + gathered_ref[shard]
    running = amplitude * running
    half = channels // 2
    kept = jnp.where(place % 2 == 0, running[:, :half], running[:, half:])
    high = kept.astype(BF16)
    packed_ref[tokens:, :half] = high
    packed_ref[tokens:, half:] = (kept - high.astype(F32)).astype(BF16)

    gate_input(k_ref, v_ref, u_ref)
    before = lax.broadcasted_iota(jnp.int32, (CHUNKS, LANES), 0).astype(F32) * float(steps)
    for tile in range(channels // LANES):
        lanes = slice(tile * LANES, (tile + 1) * LANES)
        rate = rates[:, lanes]
        pole = jnp.exp(-rate)
        poles = [row(pole, m) for m in range(modes)]
        amplitudes = [row(amplitude[:, lanes], m) for m in range(modes)]
        states = [
            entering_ref[m, :, lanes] + row(incoming[:, lanes], m) * jnp.exp(-row(rate, m) * before)
            for m in range(modes)
        ]
        skip = jnp.broadcast_to(skip_ref[:, lanes], (CHUNKS, LANES))
        for step in range(steps):
            here = u_ref[tile, pl.ds(step, CHUNKS, stride=steps), :]
            states = [p * s + here for p, s in zip(poles, states)]
            y = total([a * s for a, s in zip(amplitudes, states)] + [skip * here])
            y_ref[tile, pl.ds(step, CHUNKS, stride=steps), :] = y
        packed_ref[:tokens, lanes] = (q_ref[:, lanes].astype(F32) * y_ref[tile]).astype(BF16)


def project_kernel(width, parts, has_total, *refs):
    count = len(parts)
    blocks, weight_ref = refs[:count], refs[count]
    refs = refs[count + 1 :]
    if has_total:
        total_in_ref, final_in_ref, *refs = refs
    out_ref, final_ref = refs
    tokens, channels = out_ref.shape
    half = channels // 2
    modes = blocks[0].shape[1] - tokens
    group = lax.axis_index("ch")
    holder = lax.axis_index("ctx") // 2
    picked = final_in_ref[...] if has_total else jnp.zeros((width, modes), F32)
    sums = [total_in_ref[...]] if has_total else []
    line = lax.broadcasted_iota(jnp.int32, (width, half), 0)
    lane = lax.broadcasted_iota(jnp.int32, (width, half), 1)
    for block, (offset, first, number) in zip(blocks, parts):
        start = lax.rem(group + (offset + WINDOW), WINDOW)
        slot = holder // WINDOW - first
        here = (start == lax.rem(holder, WINDOW)) & (slot >= 0) & (slot < number)
        kept = block[jnp.clip(slot, 0, number - 1), tokens:, :]
        chosen = jnp.where((lane == line + group * width) & here, 1.0, 0.0).astype(BF16)
        for side in (kept[:, :half], kept[:, half:]):
            picked += lax.dot_general(chosen, side, (((1,), (1,)), ((), ())), preferred_element_type=F32)
        for member in range(number):
            rows = pl.ds(pl.multiple_of((start + WINDOW * (first + member)) * channels, channels), channels)
            sums.append(jnp.dot(block[member, :tokens], weight_ref[rows, :], preferred_element_type=F32))
    final_ref[...] = picked
    out_ref[...] = total(sums).astype(out_ref.dtype)


def project(width, modes, parts, blocks, weight, before=(), last=False):
    channels = weight.shape[1]
    tokens = blocks[0].shape[1] - modes
    number = sum(part[2] for part in parts)
    return pl.pallas_call(
        functools.partial(project_kernel, width, parts, bool(before)),
        out_shape=(
            jax.ShapeDtypeStruct((tokens, channels), BF16 if last else F32),
            jax.ShapeDtypeStruct((width, modes), F32),
        ),
        compiler_params=params(16),
        cost_estimate=pl.CostEstimate(
            flops=2 * number * tokens * channels * channels,
            bytes_accessed=8 * number * tokens * channels,
            transcendentals=0,
        ),
        name="project",
    )(*blocks, weight, *before)


def params(mib):
    return pltpu.CompilerParams(vmem_limit_bytes=mib * 2**20)


def body(query_gate, key_gate, values, decay_rates, residues, skip_gain, out_weight):
    tokens, channels = values.shape
    modes = decay_rates.shape[0]
    ctx_total, groups = lax.axis_size("ctx"), lax.axis_size("ch")
    tiles = channels // LANES
    members = groups // WINDOW
    width = channels // ctx_total
    assert ctx_total == 2 * groups and channels == 2 * LANES and members >= 2
    scratch = pltpu.VMEM((tiles, tokens, LANES), F32)

    own_state, entering = pl.pallas_call(
        states_kernel,
        out_shape=(
            jax.ShapeDtypeStruct((modes, channels), F32),
            jax.ShapeDtypeStruct((modes, CHUNKS, channels), F32),
        ),
        scratch_shapes=[scratch],
        compiler_params=params(56),
        name="states",
    )(key_gate, values, decay_rates)

    gathered = lax.all_gather(own_state, "ctx", axis=0)

    packed = pl.pallas_call(
        mixing_kernel,
        out_shape=jax.ShapeDtypeStruct((tokens + modes, channels), BF16),
        scratch_shapes=[scratch, scratch],
        compiler_params=params(56),
        name="mixing",
    )(query_gate, key_gate, values, decay_rates, residues, skip_gain[None, :], gathered, entering)

    far = [[one + WINDOW * member for member in range(members)] for one in range(WINDOW)]
    own = lax.all_gather(packed, "ch", axis=0, axis_index_groups=far)

    def arrive(array, offset):
        return lax.ppermute(array, "ch", [(i, (i - offset) % groups) for i in range(groups)])

    cut = members // 2
    first, second = own[:cut], own[cut:]
    above_first, below_second = arrive(first, 1), arrive(second, -1)
    above_second, below_first = arrive(second, 1), arrive(first, -1)
    far_first, far_second = arrive(above_first, 1), arrive(below_second, -1)
    run = functools.partial(project, width, modes)
    rest = members - cut
    one = run(((0, 0, members),), (own,), out_weight)
    two = run(
        ((1, 0, cut), (-1, cut, rest), (1, cut, rest), (-1, 0, cut)),
        (above_first, below_second, above_second, below_first),
        out_weight,
        one,
    )
    layer_out, final_state = run(
        ((2, 0, cut), (2, cut, rest)), (far_first, far_second), out_weight, two, last=True
    )
    return (layer_out, final_state.T)


def solution(mesh):
    return jax.shard_map(
        body,
        mesh=mesh,
        in_specs=(
            P("ctx", "ch"),
            P("ctx", "ch"),
            P("ctx", "ch"),
            P(None, "ch"),
            P(None, "ch"),
            P("ch"),
            P(None, "ch"),
        ),
        out_specs=(P("ctx", "ch"), P(None, ("ctx", "ch"))),
        check_vma=False,
    )
```

```python
import functools

import jax
import jax.numpy as jnp
from jax import lax
from jax.experimental import pallas as pl
from jax.experimental.pallas import tpu as pltpu
from jax.sharding import PartitionSpec as P

F32 = jnp.float32
BF16 = jnp.bfloat16
LANES = 128
CHUNKS = 8
WINDOW = 4


def row(array, index):
    return jnp.broadcast_to(array[index : index + 1], (CHUNKS, LANES))


def shifted(array, by):
    place = lax.broadcasted_iota(jnp.int32, (CHUNKS, LANES), 0)
    return jnp.where(place >= by, pltpu.roll(array, by, 0), 0.0)


def total(terms):
    while len(terms) > 1:
        terms = [a + b for a, b in zip(terms[::2], terms[1::2])] + terms[len(terms) // 2 * 2 :]
    return terms[0]


def spread(inputs_ref, u_ref):
    u = inputs_ref[: u_ref.shape[1]].astype(F32)
    for tile in range(u_ref.shape[0]):
        u_ref[tile] = u[:, tile * LANES : (tile + 1) * LANES]


def states_kernel(inputs_ref, filter_ref, state_ref, entering_ref, u_ref):
    channels = inputs_ref.shape[1]
    modes = state_ref.shape[0]
    steps = u_ref.shape[1] // CHUNKS
    spread(inputs_ref, u_ref)
    for tile in range(channels // LANES):
        lanes = slice(tile * LANES, (tile + 1) * LANES)
        rate = filter_ref[:modes, lanes]
        pole = jnp.exp(-rate)
        poles = [row(pole, m) for m in range(modes)]
        states = [jnp.zeros((CHUNKS, LANES), F32) for _ in range(modes)]
        for step in range(steps):
            here = u_ref[tile, pl.ds(step, CHUNKS, stride=steps), :]
            states = [p * s + here for p, s in zip(poles, states)]
        for by in (1, 2, 4):
            decay = jnp.exp(-rate * float(steps * by))
            states = [s + row(decay, m) * shifted(s, by) for m, s in enumerate(states)]
        for m in range(modes):
            state_ref[m : m + 1, lanes] = states[m][CHUNKS - 1 :]
            entering_ref[m, :, lanes] = shifted(states[m], 1)


def mixing_kernel(inputs_ref, filter_ref, gathered_ref, entering_ref, packed_ref, u_ref, y_ref):
    shards, modes, channels = gathered_ref.shape
    tokens = u_ref.shape[1]
    steps = tokens // CHUNKS
    place = lax.axis_index("ctx")
    rates, amplitude = filter_ref[:modes], filter_ref[modes : 2 * modes]
    decay = jnp.exp(-rates * float(tokens))
    running = jnp.zeros((modes, channels), F32)
    incoming = running
    for shard in range(shards):
        incoming = jnp.where(place == shard, running, incoming)
        running = decay * running + gathered_ref[shard]
    running = amplitude * running
    half = channels // 2
    kept = jnp.where(place % 2 == 0, running[:, :half], running[:, half:])
    high = kept.astype(BF16)
    packed_ref[tokens:, :half] = high
    packed_ref[tokens:, half:] = (kept - high.astype(F32)).astype(BF16)

    spread(inputs_ref, u_ref)
    before = lax.broadcasted_iota(jnp.int32, (CHUNKS, LANES), 0).astype(F32) * float(steps)
    for tile in range(channels // LANES):
        lanes = slice(tile * LANES, (tile + 1) * LANES)
        rate = rates[:, lanes]
        pole = jnp.exp(-rate)
        poles = [row(pole, m) for m in range(modes)]
        amplitudes = [row(amplitude[:, lanes], m) for m in range(modes)]
        states = [
            entering_ref[m, :, lanes] + row(incoming[:, lanes], m) * jnp.exp(-row(rate, m) * before)
            for m in range(modes)
        ]
        skip = row(filter_ref[2 * modes :, lanes], 0)
        for step in range(steps):
            here = u_ref[tile, pl.ds(step, CHUNKS, stride=steps), :]
            states = [p * s + here for p, s in zip(poles, states)]
            y = total([a * s for a, s in zip(amplitudes, states)] + [skip * here])
            y_ref[tile, pl.ds(step, CHUNKS, stride=steps), :] = y
        packed_ref[:tokens, lanes] = (inputs_ref[tokens:, lanes].astype(F32) * y_ref[tile]).astype(BF16)


def project_kernel(width, parts, has_total, *refs):
    count = len(parts)
    blocks, weight_ref = refs[:count], refs[count]
    refs = refs[count + 1 :]
    if has_total:
        total_in_ref, final_in_ref, *refs = refs
    out_ref, final_ref = refs
    tokens, channels = out_ref.shape
    half = channels // 2
    modes = blocks[0].shape[1] - tokens
    group = lax.axis_index("ch")
    holder = lax.axis_index("ctx") // 2
    picked = final_in_ref[...] if has_total else jnp.zeros((width, modes), F32)
    sums = [total_in_ref[...]] if has_total else []
    line = lax.broadcasted_iota(jnp.int32, (width, half), 0)
    lane = lax.broadcasted_iota(jnp.int32, (width, half), 1)
    for block, (offset, first, number) in zip(blocks, parts):
        start = lax.rem(group + (offset + WINDOW), WINDOW)
        slot = holder // WINDOW - first
        here = (start == lax.rem(holder, WINDOW)) & (slot >= 0) & (slot < number)
        kept = block[jnp.clip(slot, 0, number - 1), tokens:, :]
        chosen = jnp.where((lane == line + group * width) & here, 1.0, 0.0).astype(BF16)
        for side in (kept[:, :half], kept[:, half:]):
            picked += lax.dot_general(chosen, side, (((1,), (1,)), ((), ())), preferred_element_type=F32)
        for member in range(number):
            rows = pl.ds(pl.multiple_of((start + WINDOW * (first + member)) * channels, channels), channels)
            sums.append(jnp.dot(block[member, :tokens], weight_ref[rows, :], preferred_element_type=F32))
    final_ref[...] = picked
    out_ref[...] = total(sums).astype(out_ref.dtype)


def project(width, modes, parts, blocks, weight, before=(), last=False):
    channels = weight.shape[1]
    tokens = blocks[0].shape[1] - modes
    number = sum(part[2] for part in parts)
    return pl.pallas_call(
        functools.partial(project_kernel, width, parts, bool(before)),
        out_shape=(
            jax.ShapeDtypeStruct((tokens, channels), BF16 if last else F32),
            jax.ShapeDtypeStruct((width, modes), F32),
        ),
        compiler_params=params(16),
        cost_estimate=pl.CostEstimate(
            flops=2 * number * tokens * channels * channels,
            bytes_accessed=8 * number * tokens * channels,
            transcendentals=0,
        ),
        name="project",
    )(*blocks, weight, *before)


def params(mib):
    return pltpu.CompilerParams(vmem_limit_bytes=mib * 2**20)


def body(query_gate, key_gate, values, decay_rates, residues, skip_gain, out_weight):
    tokens, channels = values.shape
    modes = decay_rates.shape[0]
    ctx_total, groups = lax.axis_size("ctx"), lax.axis_size("ch")
    tiles = channels // LANES
    members = groups // WINDOW
    width = channels // ctx_total
    assert ctx_total == 2 * groups and channels == 2 * LANES and members >= 2
    scratch = pltpu.VMEM((tiles, tokens, LANES), F32)

    gated = (key_gate.astype(F32) * values.astype(F32)).astype(BF16)
    inputs = jnp.concatenate([gated, query_gate])
    amplitude = residues * jnp.sqrt(-jnp.expm1(-2.0 * decay_rates))
    filters = jnp.concatenate([decay_rates, amplitude, skip_gain[None, :]])

    own_state, entering = pl.pallas_call(
        states_kernel,
        out_shape=(
            jax.ShapeDtypeStruct((modes, channels), F32),
            jax.ShapeDtypeStruct((modes, CHUNKS, channels), F32),
        ),
        scratch_shapes=[scratch],
        compiler_params=params(16),
        name="states",
    )(inputs, filters)

    planes = [[8 * x + k for k in range(8)] for x in range(ctx_total // 8)]
    gathered = lax.all_gather(own_state, "ctx", axis=0, axis_index_groups=planes)
    columns = [[8 * x + k for x in range(ctx_total // 8)] for k in range(8)]
    gathered = lax.all_gather(gathered, "ctx", axis=0, axis_index_groups=columns).reshape(ctx_total, modes, channels)

    packed = pl.pallas_call(
        mixing_kernel,
        out_shape=jax.ShapeDtypeStruct((tokens + modes, channels), BF16),
        scratch_shapes=[scratch, scratch],
        compiler_params=params(16),
        name="mixing",
    )(inputs, filters, gathered, entering)

    far = [[one + WINDOW * member for member in range(members)] for one in range(WINDOW)]
    own = lax.all_gather(packed, "ch", axis=0, axis_index_groups=far)

    def arrive(array, offset):
        return lax.ppermute(array, "ch", [(i, (i - offset) % groups) for i in range(groups)])

    cut = members // 2
    first, second = own[:cut], own[cut:]
    above_first, below_second = arrive(first, 1), arrive(second, -1)
    above_second, below_first = arrive(second, 1), arrive(first, -1)
    far_first, far_second = arrive(above_first, 1), arrive(below_second, -1)
    run = functools.partial(project, width, modes)
    rest = members - cut
    one = run(((0, 0, members),), (own,), out_weight)
    two = run(
        ((1, 0, cut), (-1, cut, rest), (1, cut, rest), (-1, 0, cut)),
        (above_first, below_second, above_second, below_first),
        out_weight,
        one,
    )
    layer_out, final_state = run(
        ((2, 0, cut), (2, cut, rest)), (far_first, far_second), out_weight, two, last=True
    )
    return (layer_out, final_state.T)


def solution(mesh):
    return jax.shard_map(
        body,
        mesh=mesh,
        in_specs=(
            P("ctx", "ch"),
            P("ctx", "ch"),
            P("ctx", "ch"),
            P(None, "ch"),
            P(None, "ch"),
            P("ch"),
            P(None, "ch"),
        ),
        out_specs=(P("ctx", "ch"), P(None, ("ctx", "ch"))),
        check_vma=False,
    )
```

```python
import functools

import jax
import jax.numpy as jnp
from jax import lax
from jax.experimental import pallas as pl
from jax.experimental.pallas import tpu as pltpu
from jax.sharding import PartitionSpec as P

F32 = jnp.float32
BF16 = jnp.bfloat16
LANES = 128
CHUNKS = 8
PLANE = 8
WINDOW = 4


def row(array, index):
    return jnp.broadcast_to(array[index : index + 1], (CHUNKS, LANES))


def shifted(array, by):
    place = lax.broadcasted_iota(jnp.int32, (CHUNKS, LANES), 0)
    return jnp.where(place >= by, pltpu.roll(array, by, 0), 0.0)


def total(terms):
    while len(terms) > 1:
        terms = [a + b for a, b in zip(terms[::2], terms[1::2])] + terms[len(terms) // 2 * 2 :]
    return terms[0]


def spread(inputs_ref, u_ref):
    u = inputs_ref[: u_ref.shape[1]].astype(F32)
    for tile in range(u_ref.shape[0]):
        u_ref[tile] = u[:, tile * LANES : (tile + 1) * LANES]


def one_less_exp(x):
    series = jnp.ones_like(x)
    for n in range(12, 1, -1):
        series = 1.0 - x * series * (1.0 / n)
    return jnp.where(x < 0.5, x * series, 1.0 - jnp.exp(-x))


def states_kernel(inputs_ref, filter_ref, state_ref, entering_ref, u_ref):
    channels = inputs_ref.shape[1]
    modes = state_ref.shape[0]
    steps = u_ref.shape[1] // CHUNKS
    spread(inputs_ref, u_ref)
    for tile in range(channels // LANES):
        lanes = slice(tile * LANES, (tile + 1) * LANES)
        rate = filter_ref[:modes, lanes]
        pole = jnp.exp(-rate)
        poles = [row(pole, m) for m in range(modes)]
        states = [jnp.zeros((CHUNKS, LANES), F32) for _ in range(modes)]
        for step in range(steps):
            here = u_ref[tile, pl.ds(step, CHUNKS, stride=steps), :]
            states = [p * s + here for p, s in zip(poles, states)]
        for by in (1, 2, 4):
            decay = jnp.exp(-rate * float(steps * by))
            states = [s + row(decay, m) * shifted(s, by) for m, s in enumerate(states)]
        for m in range(modes):
            state_ref[m : m + 1, lanes] = states[m][CHUNKS - 1 :]
            entering_ref[m, :, lanes] = shifted(states[m], 1)


def plane_kernel(tokens, filter_ref, gathered_ref, inner_ref, plane_ref):
    shards, modes, channels = gathered_ref.shape
    place = lax.rem(lax.axis_index("ctx"), shards)
    decay = jnp.exp(-filter_ref[:modes] * float(tokens))
    running = jnp.zeros((modes, channels), F32)
    inner = running
    for shard in range(shards):
        inner = jnp.where(place == shard, running, inner)
        running = decay * running + gathered_ref[shard]
    inner_ref[...] = inner
    plane_ref[...] = running


def mixing_kernel(inputs_ref, filter_ref, inner_ref, planes_ref, entering_ref, packed_ref, u_ref, y_ref):
    planes, modes, channels = planes_ref.shape
    tokens = u_ref.shape[1]
    steps = tokens // CHUNKS
    place = lax.axis_index("ctx")
    rates = filter_ref[:modes]
    amplitude = filter_ref[modes : 2 * modes] * jnp.sqrt(one_less_exp(2.0 * rates))
    decay = jnp.exp(-rates * float(tokens * PLANE))
    running = jnp.zeros((modes, channels), F32)
    incoming = running
    for plane in range(planes):
        incoming = jnp.where(place // PLANE == plane, running, incoming)
        running = decay * running + planes_ref[plane]
    within = (lax.rem(place, PLANE) * tokens).astype(F32)
    incoming = inner_ref[...] + jnp.exp(-rates * within) * incoming
    running = amplitude * running
    half = channels // 2
    kept = jnp.where(place % 2 == 0, running[:, :half], running[:, half:])
    high = kept.astype(BF16)
    packed_ref[tokens:, :half] = high
    packed_ref[tokens:, half:] = (kept - high.astype(F32)).astype(BF16)

    spread(inputs_ref, u_ref)
    before = lax.broadcasted_iota(jnp.int32, (CHUNKS, LANES), 0).astype(F32) * float(steps)
    for tile in range(channels // LANES):
        lanes = slice(tile * LANES, (tile + 1) * LANES)
        rate = rates[:, lanes]
        pole = jnp.exp(-rate)
        poles = [row(pole, m) for m in range(modes)]
        amplitudes = [row(amplitude[:, lanes], m) for m in range(modes)]
        states = [
            entering_ref[m, :, lanes] + row(incoming[:, lanes], m) * jnp.exp(-row(rate, m) * before)
            for m in range(modes)
        ]
        skip = row(filter_ref[2 * modes :, lanes], 0)
        for step in range(steps):
            here = u_ref[tile, pl.ds(step, CHUNKS, stride=steps), :]
            states = [p * s + here for p, s in zip(poles, states)]
            y = total([a * s for a, s in zip(amplitudes, states)] + [skip * here])
            y_ref[tile, pl.ds(step, CHUNKS, stride=steps), :] = y
        packed_ref[:tokens, lanes] = (inputs_ref[tokens:, lanes].astype(F32) * y_ref[tile]).astype(BF16)


def project_kernel(width, parts, has_total, *refs):
    count = len(parts)
    blocks, weight_ref = refs[:count], refs[count]
    refs = refs[count + 1 :]
    if has_total:
        total_in_ref, final_in_ref, *refs = refs
    out_ref, final_ref = refs
    tokens, channels = out_ref.shape
    half = channels // 2
    modes = blocks[0].shape[1] - tokens
    group = lax.axis_index("ch")
    holder = lax.axis_index("ctx") // 2
    picked = final_in_ref[...] if has_total else jnp.zeros((width, modes), F32)
    sums = [total_in_ref[...]] if has_total else []
    line = lax.broadcasted_iota(jnp.int32, (width, half), 0)
    lane = lax.broadcasted_iota(jnp.int32, (width, half), 1)
    for block, (offset, first, number) in zip(blocks, parts):
        start = lax.rem(group + (offset + WINDOW), WINDOW)
        slot = holder // WINDOW - first
        here = (start == lax.rem(holder, WINDOW)) & (slot >= 0) & (slot < number)
        kept = block[jnp.clip(slot, 0, number - 1), tokens:, :]
        chosen = jnp.where((lane == line + group * width) & here, 1.0, 0.0).astype(BF16)
        for side in (kept[:, :half], kept[:, half:]):
            picked += lax.dot_general(chosen, side, (((1,), (1,)), ((), ())), preferred_element_type=F32)
        for member in range(number):
            rows = pl.ds(pl.multiple_of((start + WINDOW * (first + member)) * channels, channels), channels)
            sums.append(jnp.dot(block[member, :tokens], weight_ref[rows, :], preferred_element_type=F32))
    final_ref[...] = picked
    out_ref[...] = total(sums).astype(out_ref.dtype)


def project(width, modes, parts, blocks, weight, before=(), last=False):
    channels = weight.shape[1]
    tokens = blocks[0].shape[1] - modes
    number = sum(part[2] for part in parts)
    return pl.pallas_call(
        functools.partial(project_kernel, width, parts, bool(before)),
        out_shape=(
            jax.ShapeDtypeStruct((tokens, channels), BF16 if last else F32),
            jax.ShapeDtypeStruct((width, modes), F32),
        ),
        compiler_params=params(16),
        cost_estimate=pl.CostEstimate(
            flops=2 * number * tokens * channels * channels,
            bytes_accessed=8 * number * tokens * channels,
            transcendentals=0,
        ),
        name="project",
    )(*blocks, weight, *before)


def params(mib):
    return pltpu.CompilerParams(vmem_limit_bytes=mib * 2**20)


def body(query_gate, key_gate, values, decay_rates, residues, skip_gain, out_weight):
    tokens, channels = values.shape
    modes = decay_rates.shape[0]
    ctx_total, groups = lax.axis_size("ctx"), lax.axis_size("ch")
    tiles = channels // LANES
    members = groups // WINDOW
    width = channels // ctx_total
    assert ctx_total == 2 * groups and channels == 2 * LANES and members >= 2
    scratch = pltpu.VMEM((tiles, tokens, LANES), F32)

    gated = (key_gate.astype(F32) * values.astype(F32)).astype(BF16)
    inputs = jnp.concatenate([gated, query_gate])
    filters = jnp.concatenate([decay_rates, residues, skip_gain[None, :]])

    own_state, entering = pl.pallas_call(
        states_kernel,
        out_shape=(
            jax.ShapeDtypeStruct((modes, channels), F32),
            jax.ShapeDtypeStruct((modes, CHUNKS, channels), F32),
        ),
        scratch_shapes=[scratch],
        compiler_params=params(16),
        name="states",
    )(inputs, filters)

    rows, whole = ctx_total // PLANE, range(PLANE)
    gathered = lax.all_gather(
        own_state, "ctx", axis=0, axis_index_groups=[[PLANE * x + k for k in whole] for x in range(rows)]
    )
    inner, plane = pl.pallas_call(
        functools.partial(plane_kernel, tokens),
        out_shape=(jax.ShapeDtypeStruct((modes, channels), F32),) * 2,
        compiler_params=params(16),
        name="plane",
    )(filters, gathered)
    planes = lax.all_gather(
        plane, "ctx", axis=0, axis_index_groups=[[PLANE * x + k for x in range(rows)] for k in whole]
    )

    packed = pl.pallas_call(
        mixing_kernel,
        out_shape=jax.ShapeDtypeStruct((tokens + modes, channels), BF16),
        scratch_shapes=[scratch, scratch],
        compiler_params=params(16),
        name="mixing",
    )(inputs, filters, inner, planes, entering)

    far = [[one + WINDOW * member for member in range(members)] for one in range(WINDOW)]
    own = lax.all_gather(packed, "ch", axis=0, axis_index_groups=far)

    def arrive(array, offset):
        return lax.ppermute(array, "ch", [(i, (i - offset) % groups) for i in range(groups)])

    cut = members // 2
    first, second = own[:cut], own[cut:]
    above_first, below_second = arrive(first, 1), arrive(second, -1)
    above_second, below_first = arrive(second, 1), arrive(first, -1)
    far_first, far_second = arrive(above_first, 1), arrive(below_second, -1)
    run = functools.partial(project, width, modes)
    rest = members - cut
    one = run(((0, 0, members),), (own,), out_weight)
    two = run(
        ((1, 0, cut), (-1, cut, rest), (1, cut, rest), (-1, 0, cut)),
        (above_first, below_second, above_second, below_first),
        out_weight,
        one,
    )
    layer_out, final_state = run(
        ((2, 0, cut), (2, cut, rest)), (far_first, far_second), out_weight, two, last=True
    )
    return (layer_out, final_state.T)


def solution(mesh):
    return jax.shard_map(
        body,
        mesh=mesh,
        in_specs=(
            P("ctx", "ch"),
            P("ctx", "ch"),
            P("ctx", "ch"),
            P(None, "ch"),
            P(None, "ch"),
            P("ch"),
            P(None, "ch"),
        ),
        out_specs=(P("ctx", "ch"), P(None, ("ctx", "ch"))),
        check_vma=False,
    )
```

```python
import functools

import jax
import jax.numpy as jnp
from jax import lax
from jax.experimental import pallas as pl
from jax.experimental.pallas import tpu as pltpu
from jax.sharding import PartitionSpec as P

F32 = jnp.float32
BF16 = jnp.bfloat16
LANES = 128
CHUNKS = 8
PLANE = 8
WINDOW = 4


def row(array, index):
    return jnp.broadcast_to(array[index : index + 1], (CHUNKS, LANES))


def shifted(array, by):
    place = lax.broadcasted_iota(jnp.int32, (CHUNKS, LANES), 0)
    return jnp.where(place >= by, pltpu.roll(array, by, 0), 0.0)


def total(terms):
    while len(terms) > 1:
        terms = [a + b for a, b in zip(terms[::2], terms[1::2])] + terms[len(terms) // 2 * 2 :]
    return terms[0]


def spread(inputs_ref, u_ref):
    u = inputs_ref[: u_ref.shape[1]].astype(F32)
    for tile in range(u_ref.shape[0]):
        u_ref[tile] = u[:, tile * LANES : (tile + 1) * LANES]


def one_less_exp(x):
    series = jnp.ones_like(x)
    for n in range(12, 1, -1):
        series = 1.0 - x * series * (1.0 / n)
    return jnp.where(x < 0.5, x * series, 1.0 - jnp.exp(-x))


def states_kernel(inputs_ref, filter_ref, state_ref, entering_ref, u_ref):
    channels = inputs_ref.shape[1]
    modes = state_ref.shape[0]
    steps = u_ref.shape[1] // CHUNKS
    spread(inputs_ref, u_ref)
    for tile in range(channels // LANES):
        lanes = slice(tile * LANES, (tile + 1) * LANES)
        rate = filter_ref[:modes, lanes]
        pole = jnp.exp(-rate)
        poles = [row(pole, m) for m in range(modes)]
        states = [jnp.zeros((CHUNKS, LANES), F32) for _ in range(modes)]
        for step in range(steps):
            here = u_ref[tile, pl.ds(step, CHUNKS, stride=steps), :]
            states = [p * s + here for p, s in zip(poles, states)]
        for by in (1, 2, 4):
            decay = jnp.exp(-rate * float(steps * by))
            states = [s + row(decay, m) * shifted(s, by) for m, s in enumerate(states)]
        for m in range(modes):
            state_ref[m : m + 1, lanes] = states[m][CHUNKS - 1 :]
            entering_ref[m, :, lanes] = shifted(states[m], 1)


def plane_kernel(tokens, filter_ref, gathered_ref, inner_ref, plane_ref):
    shards, modes, channels = gathered_ref.shape
    place = lax.rem(lax.axis_index("ctx"), shards)
    decay = jnp.exp(-filter_ref[:modes] * float(tokens))
    running = jnp.zeros((modes, channels), F32)
    inner = running
    for shard in range(shards):
        inner = jnp.where(place == shard, running, inner)
        running = decay * running + gathered_ref[shard]
    inner_ref[...] = inner
    plane_ref[...] = running


def mixing_kernel(inputs_ref, filter_ref, inner_ref, planes_ref, entering_ref, packed_ref, u_ref, y_ref):
    planes, modes, channels = planes_ref.shape
    tokens = u_ref.shape[1]
    steps = tokens // CHUNKS
    place = lax.axis_index("ctx")
    rates = filter_ref[:modes]
    amplitude = filter_ref[modes : 2 * modes] * jnp.sqrt(one_less_exp(2.0 * rates))
    decay = jnp.exp(-rates * float(tokens * PLANE))
    running = jnp.zeros((modes, channels), F32)
    incoming = running
    for plane in range(planes):
        incoming = jnp.where(place // PLANE == plane, running, incoming)
        running = decay * running + planes_ref[plane]
    within = (lax.rem(place, PLANE) * tokens).astype(F32)
    incoming = inner_ref[...] + jnp.exp(-rates * within) * incoming
    running = amplitude * running
    half = channels // 2
    kept = jnp.where(place % 2 == 0, running[:, :half], running[:, half:])
    high = kept.astype(BF16)
    packed_ref[tokens:, :half] = high
    packed_ref[tokens:, half:] = (kept - high.astype(F32)).astype(BF16)

    spread(inputs_ref, u_ref)
    before = lax.broadcasted_iota(jnp.int32, (CHUNKS, LANES), 0).astype(F32) * float(steps)
    for tile in range(channels // LANES):
        lanes = slice(tile * LANES, (tile + 1) * LANES)
        rate = rates[:, lanes]
        pole = jnp.exp(-rate)
        poles = [row(pole, m) for m in range(modes)]
        amplitudes = [row(amplitude[:, lanes], m) for m in range(modes)]
        states = [
            entering_ref[m, :, lanes] + row(incoming[:, lanes], m) * jnp.exp(-row(rate, m) * before)
            for m in range(modes)
        ]
        skip = row(filter_ref[2 * modes :, lanes], 0)
        for step in range(steps):
            here = u_ref[tile, pl.ds(step, CHUNKS, stride=steps), :]
            states = [p * s + here for p, s in zip(poles, states)]
            y = total([a * s for a, s in zip(amplitudes, states)] + [skip * here])
            y_ref[tile, pl.ds(step, CHUNKS, stride=steps), :] = y
        packed_ref[:tokens, lanes] = (inputs_ref[tokens:, lanes].astype(F32) * y_ref[tile]).astype(BF16)


def project_kernel(width, parts, has_total, *refs):
    count = len(parts)
    blocks, weight_ref = refs[:count], refs[count]
    refs = refs[count + 1 :]
    if has_total:
        total_in_ref, final_in_ref, *refs = refs
    out_ref, final_ref = refs
    tokens, channels = out_ref.shape
    half = channels // 2
    modes = blocks[0].shape[1] - tokens
    group = lax.axis_index("ch")
    holder = lax.axis_index("ctx") // 2
    picked = final_in_ref[...] if has_total else jnp.zeros((width, modes), F32)
    sums = [total_in_ref[...]] if has_total else []
    line = lax.broadcasted_iota(jnp.int32, (width, half), 0)
    lane = lax.broadcasted_iota(jnp.int32, (width, half), 1)
    for block, (offset, first, number) in zip(blocks, parts):
        start = lax.rem(group + (offset + WINDOW), WINDOW)
        slot = holder // WINDOW - first
        here = (start == lax.rem(holder, WINDOW)) & (slot >= 0) & (slot < number)
        kept = block[jnp.clip(slot, 0, number - 1), tokens:, :]
        chosen = jnp.where((lane == line + group * width) & here, 1.0, 0.0).astype(BF16)
        for side in (kept[:, :half], kept[:, half:]):
            picked += lax.dot_general(chosen, side, (((1,), (1,)), ((), ())), preferred_element_type=F32)
        for member in range(number):
            rows = pl.ds(pl.multiple_of((start + WINDOW * (first + member)) * channels, channels), channels)
            sums.append(jnp.dot(block[member, :tokens], weight_ref[rows, :], preferred_element_type=F32))
    final_ref[...] = picked
    out_ref[...] = total(sums).astype(out_ref.dtype)


def project(width, modes, parts, blocks, weight, before=(), last=False):
    channels = weight.shape[1]
    tokens = blocks[0].shape[1] - modes
    number = sum(part[2] for part in parts)
    return pl.pallas_call(
        functools.partial(project_kernel, width, parts, bool(before)),
        out_shape=(
            jax.ShapeDtypeStruct((tokens, channels), BF16 if last else F32),
            jax.ShapeDtypeStruct((width, modes), F32),
        ),
        compiler_params=params(16),
        cost_estimate=pl.CostEstimate(
            flops=2 * number * tokens * channels * channels,
            bytes_accessed=8 * number * tokens * channels,
            transcendentals=0,
        ),
        name="project",
    )(*blocks, weight, *before)


def params(mib):
    return pltpu.CompilerParams(vmem_limit_bytes=mib * 2**20)


def body(query_gate, key_gate, values, decay_rates, residues, skip_gain, out_weight):
    tokens, channels = values.shape
    modes = decay_rates.shape[0]
    ctx_total, groups = lax.axis_size("ctx"), lax.axis_size("ch")
    tiles = channels // LANES
    members = groups // WINDOW
    width = channels // ctx_total
    assert ctx_total == 2 * groups and channels == 2 * LANES and members >= 2
    scratch = pltpu.VMEM((tiles, tokens, LANES), F32)

    gated = (key_gate.astype(F32) * values.astype(F32)).astype(BF16)
    inputs = jnp.concatenate([gated, query_gate])
    filters = jnp.concatenate([decay_rates, residues, skip_gain[None, :]])

    own_state, entering = pl.pallas_call(
        states_kernel,
        out_shape=(
            jax.ShapeDtypeStruct((modes, channels), F32),
            jax.ShapeDtypeStruct((modes, CHUNKS, channels), F32),
        ),
        scratch_shapes=[scratch],
        compiler_params=params(16),
        name="states",
    )(inputs, filters)

    rows, whole = ctx_total // PLANE, range(PLANE)
    gathered = lax.all_gather(
        own_state, "ctx", axis=0, axis_index_groups=[[PLANE * x + k for k in whole] for x in range(rows)]
    )
    inner, plane = pl.pallas_call(
        functools.partial(plane_kernel, tokens),
        out_shape=(jax.ShapeDtypeStruct((modes, channels), F32),) * 2,
        compiler_params=params(16),
        name="plane",
    )(filters, gathered)
    planes = lax.all_gather(
        plane, "ctx", axis=0, axis_index_groups=[[PLANE * x + k for x in range(rows)] for k in whole]
    )

    packed = pl.pallas_call(
        mixing_kernel,
        out_shape=jax.ShapeDtypeStruct((tokens + modes, channels), BF16),
        scratch_shapes=[scratch, scratch],
        compiler_params=params(16),
        name="mixing",
    )(inputs, filters, inner, planes, entering)

    far = [[one + WINDOW * member for member in range(members)] for one in range(WINDOW)]
    own = lax.all_gather(packed, "ch", axis=0, axis_index_groups=far)

    def arrive(array, offset):
        return lax.ppermute(array, "ch", [(i, (i - offset) % groups) for i in range(groups)])

    cut = members // 2
    first, second = own[:cut], own[cut:]
    above_first, below_second = arrive(first, 1), arrive(second, -1)
    above_second, below_first = arrive(second, 1), arrive(first, -1)
    far_first, far_second = arrive(above_first, 1), arrive(below_second, -1)
    run = functools.partial(project, width, modes)
    rest = members - cut
    one = run(((0, 0, members),), (own,), out_weight)
    two = run(((1, 0, cut), (-1, cut, rest)), (above_first, below_second), out_weight, one)
    layer_out, final_state = run(
        ((1, cut, rest), (-1, 0, cut), (2, 0, cut), (2, cut, rest)),
        (above_second, below_first, far_first, far_second),
        out_weight,
        two,
        last=True,
    )
    return (layer_out, final_state.T)


def solution(mesh):
    return jax.shard_map(
        body,
        mesh=mesh,
        in_specs=(
            P("ctx", "ch"),
            P("ctx", "ch"),
            P("ctx", "ch"),
            P(None, "ch"),
            P(None, "ch"),
            P("ch"),
            P(None, "ch"),
        ),
        out_specs=(P("ctx", "ch"), P(None, ("ctx", "ch"))),
        check_vma=False,
    )
```
